512 devices in a mesh: kx: 8 (over z), ky: 8 (over y_hi, core), kz: 8 (over y_lo, x).
Axes of the slice: x: 4, y: 8 (y_hi: 4, y_lo: 2; y = y_hi * 2 + y_lo), z: 8, core: 2. Of those that a mesh axis runs over, the one named last changes fastest.
Arguments:
- target: bfloat16 [8, 8, 8, 8, 4096], P('kx', 'ky', 'kz'), may hold values from -6 to 6
- target_energy: bfloat16 [8, 8, 8, 8], P('kx', 'ky', 'kz'), may hold values from -1 to 1
- waves: bfloat16 [8, 8, 8, 128, 4096], P('kx', 'ky', 'kz'), may hold values from -6 to 6
- band_energy: float32 [8, 8, 8, 128], P('kx', 'ky', 'kz'), may hold values from -3 to 3
- occupation: int32 [8, 8, 8, 128], P('kx', 'ky', 'kz'), may hold values 0 or 1
- gmap: int32 [3, 4096], replicated, may hold values from 0 to 4095, each once within a row
- pole_vectors: bfloat16 [8, 8, 8, 256, 4096], P('kx', 'ky', 'kz'), may hold values from -0.09375 to 0.09375
- pole_freq: bfloat16 [8, 8, 8, 256], P('kx', 'ky', 'kz'), may hold values from 0.5 to 3
- pole_weight: bfloat16 [8, 8, 8, 256], P('kx', 'ky', 'kz'), may hold values from 0.19921875 to 2
Outputs:
- sigma: float32 [8, 8, 8, 8, 256], P('kx', 'ky', 'kz')
The draws below stay inside these ranges and needn't reach their ends.
Inputs may be any that keep to these rules, and one draw needn't show every extreme that they name: Each row of gmap is a permutation of 0 to 4095.
All inputs are finite; a program needn't handle non-finite values. No bound on the sum of `occupation` on one device may be relied on, other than what follows from the above.
Results may differ from the reference program's by a relative error of at most 0.00057.
Values may be sent and summed in bfloat16 or wider, within the bound.
A program may use at most 64 MiB of HBM per device.

```python
import math
import jax
import jax.numpy as jnp
from jax import lax

M_TGT = 8
NSUM = 128
NPOLE = 256
NPW = 4096
Q = 3
NKX = 8
NKY = 8
NKZ = 8


def with_ends(result, key, low, top_value):
    place = [jax.random.randint(jax.random.fold_in(key, axis), (), 0, length) for axis, length in enumerate(result.shape)]
    widest = result.shape.index(max(result.shape))
    next_to = place[:widest] + [(place[widest] + 1) % result.shape[widest]] + place[widest + 1:]
    return result.at[tuple(place)].set(low).at[tuple(next_to)].set(top_value)


def shard_levels(rng, dims, cuts, low, top_value):
    factor_of = 1.0
    for axis_at, blocks in cuts:
        draws = jax.random.uniform(jax.random.fold_in(jax.random.fold_in(rng, 6), axis_at), (blocks,), jnp.float32, low / len(cuts), top_value / len(cuts))
        factor_of = factor_of * jnp.repeat(jnp.exp(draws), dims[axis_at] // blocks).reshape((-1,) + (1,) * (len(dims) - 1 - axis_at))
    return factor_of


def bell_draw(key, extent, scale, limit, cuts=(), dtype=jnp.bfloat16):
    loudness = shard_levels(key, extent, cuts, -0.22, 0.18) if cuts else 1.0
    entries = jax.random.normal(key, extent, jnp.float32) * scale * loudness
    return jnp.minimum(jnp.maximum(entries, -limit), limit).astype(dtype)


def setup_inputs(seed: int = 0) -> dict:
    streams_of = jax.random.split(jax.random.key(seed), 10)
    return {
        "target": bell_draw(streams_of[0], (NKX, NKY, NKZ, M_TGT, NPW), 1.0, 6.0, ((0, 8), (1, 8), (2, 8))),
        "target_energy": jnp.clip(jax.random.uniform(streams_of[1], (NKX, NKY, NKZ, M_TGT), jnp.float32, -1.0, 1.0) * shard_levels(streams_of[1], (NKX, NKY, NKZ, M_TGT), ((0, 8), (1, 8), (2, 8)), -0.4, 0.0), -1.0, 1.0).astype(jnp.bfloat16),
        "waves": bell_draw(streams_of[2], (NKX, NKY, NKZ, NSUM, NPW), 1.0, 6.0, ((0, 8), (1, 8), (2, 8))),
        "band_energy": jnp.clip(jax.random.uniform(streams_of[3], (NKX, NKY, NKZ, NSUM), jnp.float32, -3.0, 3.0) * shard_levels(streams_of[3], (NKX, NKY, NKZ, NSUM), ((0, 8), (1, 8), (2, 8)), -0.4, 0.0), -3.0, 3.0),
        "occupation": with_ends((jax.random.randint(streams_of[4], (NKX, NKY, NKZ, NSUM), 0, 2) < 1).astype(jnp.int32), jax.random.fold_in(streams_of[4], 1), 0, 1),
        "gmap": jax.vmap(lambda own: jax.random.permutation(own, NPW))(jax.random.split(streams_of[5], Q)).reshape((Q, NPW)).astype(jnp.int32),
        "pole_vectors": bell_draw(streams_of[6], (NKX, NKY, NKZ, NPOLE, NPW), NPW ** -0.5, 0.09375, ((0, 8), (1, 8), (2, 8))),
        "pole_freq": jnp.clip(jnp.exp(math.log(3.0) - 1.7917595 * jax.random.uniform(streams_of[7], (NKX, NKY, NKZ, NPOLE), jnp.float32) ** shard_levels(streams_of[7], (NKX, NKY, NKZ, NPOLE), ((0, 8), (1, 8), (2, 8)), -0.2, 0.2)), 0.5, 3.0).astype(jnp.bfloat16),
        "pole_weight": jnp.clip(jnp.exp(math.log(2.0) - 2.306499 * jax.random.uniform(streams_of[8], (NKX, NKY, NKZ, NPOLE), jnp.float32) ** shard_levels(streams_of[8], (NKX, NKY, NKZ, NPOLE), ((0, 8), (1, 8), (2, 8)), -0.2, 0.2)), 0.19921875, 2.0).astype(jnp.bfloat16),
    }


QSTEPS = ((1, 0, 0), (1, 1, 0), (1, 1, 1))


def contribution(tgt, energy, wav, lvl, perm, vecs, freq, weight):
    cols = jnp.take(wav, perm, axis=1)
    pair = (tgt.astype(jnp.float32)[:, None, :] * cols.astype(jnp.float32)[None, :, :]).astype(jnp.bfloat16)
    pair = pair.reshape(tgt.shape[0] * wav.shape[0], tgt.shape[1])
    proj = lax.dot_general(pair, vecs, (((1,), (1,)), ((), ())), preferred_element_type=jnp.float32)
    proj = proj.reshape(tgt.shape[0], wav.shape[0], vecs.shape[0])
    gap = energy.astype(jnp.float32)[:, None] - lvl.astype(jnp.float32)[None, :]
    freq32 = freq.astype(jnp.float32)
    factor = weight.astype(jnp.float32) * freq32 / (freq32 * freq32 + gap[:, :, None] * gap[:, :, None])
    return jnp.sum(proj * proj * factor, axis=1)


def reference(target, target_energy, waves, band_energy, occupation, gmap, pole_vectors, pole_freq, pole_weight):
    nx, ny, nz = waves.shape[0], waves.shape[1], waves.shape[2]
    count = nx * ny * nz
    level = (band_energy - (2 * occupation - 1).astype(jnp.float32)).astype(jnp.bfloat16)
    tflat = target.reshape(count, target.shape[3], target.shape[4])
    eflat = target_energy.reshape(count, target_energy.shape[3])
    total = jnp.zeros((count, target.shape[3], pole_vectors.shape[3]), jnp.float32)
    for step, (qx, qy, qz) in enumerate(QSTEPS):
        wshift = jnp.roll(waves, (qx, qy, qz), axis=(0, 1, 2)).reshape(count, waves.shape[3], waves.shape[4])
        lshift = jnp.roll(level, (qx, qy, qz), axis=(0, 1, 2)).reshape(count, level.shape[3])
        vecs = pole_vectors[qx, qy, qz]
        freq = pole_freq[qx, qy, qz]
        weight = pole_weight[qx, qy, qz]
        perm = gmap[step]

        def single(items):
            return contribution(items[0], items[1], items[2], items[3], perm, vecs, freq, weight)

        total = total + lax.map(single, (tflat, eflat, wshift, lshift))
    total = total / jnp.float32(waves.shape[3])
    return total.reshape(nx, ny, nz, target.shape[3], pole_vectors.shape[3])
```

```python
import functools

import jax
import jax.numpy as jnp
from jax import lax
from jax.experimental import pallas as pl
from jax.experimental.pallas import tpu as pltpu
from jax.sharding import PartitionSpec as P

MESH = pl.DeviceIdType.MESH
QSTEPS = ((1, 0, 0), (1, 1, 0), (1, 1, 1))
NQ = 3
BLK = 256
SUB = 4
ROWS = BLK // SUB
EXTRA = 16
NEAR = {1: (0, 1, 0), 2: (1, 0, 0), 3: (0, 0, 1), 5: (0, 0, -1), 6: (-1, 0, 0), 7: (0, -1, 0)}
FAR = ((2, 0, 0), (0, 1, 1), (0, -1, -1))
WAY = [[FAR[s] if t == 4 else NEAR[t] for s in range(NQ)] for t in range(1, 8)]


def chip_of(me):
    kx, ky, kz = me
    return kz % 4, (ky // 2) * 2 + kz // 4, kx, ky % 2


def device_of(x, y, z, c):
    return z, (y // 2) * 2 + c, (y % 2) * 4 + x


def kernel(
    gmap, vecs, waves, target, energy_row, band_energy, occupation, freq_row, weight_row, out,
    held, made, onehot, own, sent, tgt, moved, total, factor, answer, part, level, pole,
    own_sem, ss1, ss2, ss3, ss4, sst, ssr, rs2, rs3, rs4, rst, rsr,
):
    me = tuple(lax.axis_index(a) for a in ("kx", "ky", "kz"))
    x, y, z, c = chip_of(me)
    cls = (2 * x + y + 3 * z) % 8
    mine = cls + 8 * c

    def chip(dx, dy, dz, core=c):
        return device_of((x + dx + 4) % 4, (y + dy + 8) % 8, (z + dz + 8) % 8, core)

    def shifted(q, sign):
        return tuple((i + sign * d + 8) % 8 for i, d in zip(me, q))

    sibling = chip(0, 0, 0, 1 - c)
    is_source = (z == 1) & (y == 0) & ((x == 0) | ((x == 1) & (c == 1)))
    source_q = jnp.where(x == 0, c, 2)
    held_q = ((z + 8 - 4 * c) % 8) // 3
    is_holder = (z + 8 - 4 * c) % 8 == 3 * held_q

    barrier = pltpu.get_barrier_semaphore()

    def hello(device):
        pl.semaphore_signal(barrier, inc=1, device_id=device, device_id_type=MESH)

    for q in QSTEPS:
        hello(shifted(q, 1))
        hello(shifted(q, -1))
    hello(sibling)
    for t in range(7):
        for way in sorted(set(WAY[t])):
            hello(chip(-way[0], -way[1], -way[2]))

    def greet(i, _):
        s, hx = i // 4, i % 4
        hz = (3 * s + 4 * c) % 8
        hy = (cls + 48 - 2 * hx - 3 * hz) % 8

        @pl.when(jnp.logical_not((hx == x) & (hz == z)))
        def _():
            hello(device_of(hx, hy, hz, c))

        return 0

    lax.fori_loop(0, NQ * SUB, greet, 0)

    @pl.when(is_holder)
    def _():
        hello(device_of(jnp.where(held_q == 2, 1, 0), 0, 1, jnp.where(held_q == 0, 0, 1)))

    load = pltpu.make_async_copy(vecs, own, own_sem)

    @pl.when(is_source)
    def _():
        load.start()

    def wanted(q):
        row = gmap[pl.ds(q, 1), :]
        return row // BLK, row % BLK

    def fill_onehot(low):
        for r in range(0, BLK, 32):
            rows = lax.broadcasted_iota(jnp.int32, (32, low.shape[1]), 0) + r
            onehot[r : r + 32, :] = jnp.where(rows == low, 1.0, 0.0).astype(jnp.bfloat16)

    sent[:, : target.shape[1]] = target[...].astype(jnp.float32)
    spot = lax.broadcasted_iota(jnp.int32, (8, 8), 0) == lax.broadcasted_iota(jnp.int32, (8, 8), 1)
    spot = jnp.where(spot, jnp.broadcast_to(energy_row[...].astype(jnp.float32), (8, 8)), 0.0)
    sent[:, target.shape[1] :] = jnp.broadcast_to(jnp.sum(spot, axis=1, keepdims=True), (8, 128))
    lvl_row = band_energy[...] - (2 * occupation[...] - 1).astype(jnp.float32)
    lvl_row = lvl_row.astype(jnp.bfloat16).astype(jnp.float32)
    level[...] = jnp.broadcast_to(lvl_row, (128, 128)).T
    row_at = lax.broadcasted_iota(jnp.int32, (EXTRA, 256), 0)
    pole[...] = jnp.where(
        row_at == 0,
        freq_row[...].astype(jnp.float32),
        jnp.where(row_at == 1, weight_row[...].astype(jnp.float32), 0.0),
    ).astype(jnp.bfloat16)

    peers = 2 * NQ + 1 + 9
    pl.semaphore_wait(barrier, peers + jnp.where(is_holder, 31, 0) + jnp.where(is_source, 16 * SUB, 0))

    def target_copy(s):
        return pltpu.make_async_remote_copy(
            sent, tgt.at[s], sst.at[s], rst.at[s], device_id=shifted(QSTEPS[s], -1), device_id_type=MESH
        )

    @pl.when(is_source)
    def _():
        load.wait()
        high, low = wanted(source_q)
        fill_onehot(low)

        def hand_out(pos, _):
            j = pos // 2 + 8 * (pos % 2)
            dest_c = pos % 2
            dest_cls = pos // 2
            mask = jnp.where(high == j, 1.0, 0.0).astype(jnp.bfloat16)
            block = lax.dot_general(
                onehot[...], own[...] * mask, (((1,), (1,)), ((), ())), preferred_element_type=jnp.float32
            )
            made[j, :BLK, :] = block.astype(jnp.bfloat16)
            made[j, BLK:, :] = pole[...]
            hz = (3 * source_q + 4 * dest_c) % 8
            for u in range(SUB):
                hy = (dest_cls + 48 - 2 * u - 3 * hz) % 8
                rows = pl.ds(u * ROWS, ROWS + (EXTRA if u == SUB - 1 else 0))
                pltpu.make_async_remote_copy(
                    made.at[j, rows], held.at[source_q, j, rows], ss1.at[j, u], rs2.at[source_q, u],
                    device_id=device_of(u, hy, hz, dest_c), device_id_type=MESH,
                ).start()
            return 0

        lax.fori_loop(0, 16, hand_out, 0)

    for s in range(NQ):
        target_copy(s).start()

    def permute_target(s, _):
        high, low = wanted(s)
        fill_onehot(low)
        pltpu.make_async_remote_copy(
            sent, tgt.at[s], sst.at[s], rst.at[s], device_id=sibling, device_id_type=MESH
        ).wait_recv()
        t = tgt[s, :, : target.shape[1]]
        rows = jnp.concatenate([jnp.where(high == j, t, 0.0).astype(jnp.bfloat16) for j in range(16)], axis=0)
        ordered = lax.dot_general(
            rows, onehot[...], (((1,), (1,)), ((), ())), preferred_element_type=jnp.float32
        )
        for j in range(16):
            moved[s, j] = ordered[8 * j : 8 * j + 8, :]
        return 0

    lax.fori_loop(0, NQ, permute_target, 0)

    def part_copy(s, u, slot, device):
        n = ROWS + (EXTRA if u == SUB - 1 else 0)
        rows = pl.ds(u * ROWS, n)
        return pltpu.make_async_remote_copy(
            held.at[s, mine, rows], held.at[s, mine, rows], ss2.at[slot], rs2.at[s, u],
            device_id=device, device_id_type=MESH,
        )

    @pl.when(is_holder)
    def _():
        for u in range(SUB):

            @pl.when(x == u)
            def _():
                part_copy(held_q, u, 0, sibling).wait_recv()

                def give(i, _):
                    dx, dz = (i + 1) % 4, (i + 1) // 4
                    dy = (64 - 2 * dx - 3 * dz) % 8
                    part_copy(held_q, u, i, chip(dx, dy, dz)).start()
                    return 0

                lax.fori_loop(0, 31, give, 0)

    total[...] = jnp.zeros_like(total)

    def near_copy(s, t):
        return pltpu.make_async_remote_copy(
            held.at[s, mine, pl.ds(0, BLK)], held.at[s, mine, pl.ds(0, BLK)], ss3.at[s, t], rs3.at[s, cls],
            device_id=chip(*WAY[t][s]), device_id_type=MESH,
        )

    def chunk_in(s, k, sem):
        j = k + 8 * c
        return pltpu.make_async_remote_copy(
            held.at[s, j, pl.ds(0, BLK)], held.at[s, j, pl.ds(0, BLK)], ss3.at[0, 0], sem,
            device_id=sibling, device_id_type=MESH,
        )

    def side_copy(s, k):
        j = k + 8 * c
        return pltpu.make_async_remote_copy(
            held.at[s, j, pl.ds(0, BLK)], held.at[s, j, pl.ds(0, BLK)], ss4.at[s, k], rs4.at[s, k],
            device_id=sibling, device_id_type=MESH,
        )

    def side_in(s, k):
        j = k + 8 * (1 - c)
        return pltpu.make_async_remote_copy(
            held.at[s, j, pl.ds(0, BLK)], held.at[s, j, pl.ds(0, BLK)], ss4.at[s, k], rs4.at[s, k],
            device_id=sibling, device_id_type=MESH,
        )

    def spread(s):
        for u in range(SUB):

            @pl.when(jnp.logical_not(is_holder & (held_q == s) & (x == u)))
            def _():
                part_copy(s, u, 0, sibling).wait_recv()

        for t in range(7):
            near_copy(s, t).start()

    def make_factor(s):
        freq = held[s, mine, BLK : BLK + EXTRA, :].astype(jnp.float32)
        f, w = freq[0:1, :], freq[1:2, :]
        wf, ff = w * f, f * f
        e = tgt[s, :, target.shape[1] :]
        lvl = level[...]
        for m in range(8):
            gap = e[m : m + 1, :] - lvl
            gap = gap * gap
            gap = jnp.concatenate([gap, gap], axis=1)
            factor[s, m * 128 : m * 128 + 128, :] = wf / (ff + gap)

    def work(s, j):
        w = waves[:, pl.ds(pl.multiple_of(j * BLK, BLK), BLK)].astype(jnp.float32)
        t = moved[s, j]
        pair = jnp.concatenate([(t[m : m + 1, :] * w).astype(jnp.bfloat16) for m in range(8)], axis=0)
        total[s] += jnp.dot(pair, held[s, j, :BLK, :], preferred_element_type=jnp.float32)

    due = jnp.maximum(cls - 4, 0)

    def turn(k, _):
        @pl.when(k == due)
        def _():
            for s in range(NQ):
                spread(s)
            for s in range(NQ):
                make_factor(s)

        def arrive(s, _):
            @pl.when(k != cls)
            def _():
                chunk_in(s, k, rs3.at[s, k]).wait_recv()

            side_copy(s, k).start()
            work(s, k + 8 * c)
            return 0

        lax.fori_loop(0, NQ, arrive, 0)

        def arrive_side(s, _):
            side_in(s, k).wait_recv()
            work(s, k + 8 * (1 - c))
            return 0

        lax.fori_loop(0, NQ, arrive_side, 0)
        return 0

    lax.fori_loop(0, 8, turn, 0)

    def answer_copy(s):
        return pltpu.make_async_remote_copy(
            answer.at[s], part.at[s], ssr.at[s], rsr.at[s], device_id=shifted(QSTEPS[s], 1), device_id_type=MESH
        )

    for s in range(NQ):
        for m in range(8):
            rows = slice(m * 128, m * 128 + 128)
            proj = total[s, rows, :]
            answer[s, m : m + 1, :] = jnp.sum(proj * proj * factor[s, rows, :], axis=0, keepdims=True)
        answer_copy(s).start()

    for s in range(NQ):
        target_copy(s).wait_send()
        for t in range(7):
            near_copy(s, t).wait_send()

    def side_left(k, _):
        for s in range(NQ):
            side_copy(s, k).wait_send()
        return 0

    lax.fori_loop(0, 8, side_left, 0)

    @pl.when(is_holder)
    def _():
        for u in range(SUB):

            @pl.when(x == u)
            def _():
                def left(i, _):
                    part_copy(held_q, u, i, sibling).wait_send()
                    return 0

                lax.fori_loop(0, 31, left, 0)

    @pl.when(is_source)
    def _():
        def left(j, _):
            for u in range(SUB):
                rows = pl.ds(u * ROWS, ROWS + (EXTRA if u == SUB - 1 else 0))
                pltpu.make_async_remote_copy(
                    made.at[j, rows], held.at[source_q, j, rows], ss1.at[j, u], rs2.at[source_q, u],
                    device_id=sibling, device_id_type=MESH,
                ).wait_send()
            return 0

        lax.fori_loop(0, 16, left, 0)

    for s in range(NQ):
        answer_copy(s).wait()
    out[...] = (part[0] + part[1] + part[2]) * (1.0 / 128.0)


def local(target, target_energy, waves, band_energy, occupation, gmap, pole_vectors, pole_freq, pole_weight):
    tgt = target[0, 0, 0]
    vmem = pl.BlockSpec(memory_space=pltpu.VMEM)
    dma = pltpu.SemaphoreType.DMA
    out = pl.pallas_call(
        kernel,
        out_shape=jax.ShapeDtypeStruct((8, 256), jnp.float32),
        in_specs=[vmem, pl.BlockSpec(memory_space=pl.ANY)] + [vmem] * 7,
        out_specs=vmem,
        scratch_shapes=[
            pltpu.VMEM((NQ, 16, BLK + EXTRA, 256), jnp.bfloat16),
            pltpu.VMEM((16, BLK + EXTRA, 256), jnp.bfloat16),
            pltpu.VMEM((BLK, 4096), jnp.bfloat16),
            pltpu.VMEM((256, 4096), jnp.bfloat16),
            pltpu.VMEM((8, 4096 + 128), jnp.float32),
            pltpu.VMEM((NQ, 8, 4096 + 128), jnp.float32),
            pltpu.VMEM((NQ, 16, 8, BLK), jnp.float32),
            pltpu.VMEM((NQ, 1024, 256), jnp.float32),
            pltpu.VMEM((NQ, 1024, 256), jnp.float32),
            pltpu.VMEM((NQ, 8, 256), jnp.float32),
            pltpu.VMEM((NQ, 8, 256), jnp.float32),
            pltpu.VMEM((128, 128), jnp.float32),
            pltpu.VMEM((EXTRA, 256), jnp.bfloat16),
            dma,
            dma((16, SUB)),
            dma((31,)),
            dma((NQ, 7)),
            dma((NQ, 8)),
            dma((NQ,)),
            dma((NQ,)),
            dma((NQ, SUB)),
            dma((NQ, 8)),
            dma((NQ, 8)),
            dma((NQ,)),
            dma((NQ,)),
        ],
        compiler_params=pltpu.CompilerParams(
            collective_id=0, has_side_effects=True, vmem_limit_bytes=56 << 20
        ),
    )(
        gmap, pole_vectors[0, 0, 0], waves[0, 0, 0], tgt, target_energy[0, 0], band_energy[0, 0],
        occupation[0, 0], pole_freq[0, 0], pole_weight[0, 0],
    )
    return out[None, None, None]


def solution(mesh):
    cut = P("kx", "ky", "kz", None, None)
    row = P("kx", "ky", "kz", None)
    return jax.shard_map(
        local,
        mesh=mesh,
        in_specs=(cut, row, cut, row, row, P(), cut, row, row),
        out_specs=cut,
        check_vma=False,
    )
```

```python
import functools

import jax
import jax.numpy as jnp
from jax import lax
from jax.experimental import pallas as pl
from jax.experimental.pallas import tpu as pltpu
from jax.sharding import PartitionSpec as P

MESH = pl.DeviceIdType.MESH
QSTEPS = ((1, 0, 0), (1, 1, 0), (1, 1, 1))
NQ = 3
BLK = 256
SUB = 4
ROWS = BLK // SUB
AHEAD = 8
EXTRA = 16
NEAR = {1: (0, 1, 0), 2: (1, 0, 0), 3: (0, 0, 1), 5: (0, 0, -1), 6: (-1, 0, 0), 7: (0, -1, 0)}
FAR = ((2, 0, 0), (0, 1, 1), (0, -1, -1))
WAY = [[FAR[s] if t == 4 else NEAR[t] for s in range(NQ)] for t in range(1, 8)]


def chip_of(me):
    kx, ky, kz = me
    return kz % 4, (ky // 2) * 2 + kz // 4, kx, ky % 2


def device_of(x, y, z, c):
    return z, (y // 2) * 2 + c, (y % 2) * 4 + x


def kernel(
    gmap, vecs, waves, target, energy_row, band_energy, occupation, freq_row, weight_row, out,
    held, made, onehot, own, sent, tgt, moved, total, factor, answer, part, level, pole,
    own_sem, ss1, ss2, ss3, ss4, sst, ssr, rs1, rs2, rs3, rs4, rst, rsr, ready,
):
    me = tuple(lax.axis_index(a) for a in ("kx", "ky", "kz"))
    x, y, z, c = chip_of(me)
    cls = (2 * x + y + 3 * z) % 8
    mine = cls + 8 * c

    def chip(dx, dy, dz, core=c):
        return device_of((x + dx + 4) % 4, (y + dy + 8) % 8, (z + dz + 8) % 8, core)

    def shifted(q, sign):
        return tuple((i + sign * d + 8) % 8 for i, d in zip(me, q))

    sibling = chip(0, 0, 0, 1 - c)
    is_source = (z == 1) & (y == 0) & ((x == 0) | ((x == 1) & (c == 1)))
    source_q = jnp.where(x == 0, c, 2)
    late = z >= 4
    early = jnp.logical_not(late)
    held_at = (z + 7 - 4 * c) % 8
    held_q = jnp.minimum(held_at // 2, 2)
    is_holder = (held_at == 0) | (held_at == 2) | (held_at == 5)
    relay_no = jnp.where(z == 2, 3 - c, jnp.where(x == 3, 0, 1))
    is_relay = (y == 0) & (((x == 0) & (z == 2)) | ((z == 1) & (((x == 3) & (c == 1)) | ((x == 1) & (c == 0)))))
    gives = (is_source & (source_q != 1)) | is_relay

    def first_z(s, core):
        return (1 + 2 * s + s // 2 + 4 * core) % 8

    def relay_of(k):
        r = k // 2
        return device_of(
            jnp.where(r == 0, 3, jnp.where(r == 1, 1, 0)),
            0,
            jnp.where(r < 2, 1, 2),
            jnp.where((r == 0) | (r == 2), 1, 0),
        )

    def source_of(s):
        return device_of(jnp.where(s == 2, 1, 0), 0, 1, jnp.where(s == 0, 0, 1))

    def holder_of(s, u, k, core):
        hz = first_z(s, core)
        return u, (k + 48 - 2 * u - 3 * hz) % 8, hz

    def giver_of_mine():
        to_relay = held_q == 1
        return tuple(jnp.where(to_relay, a, b) for a, b in zip(relay_of(cls), source_of(held_q)))

    barrier = pltpu.get_barrier_semaphore()

    def hello(device):
        pl.semaphore_signal(barrier, inc=1, device_id=device, device_id_type=MESH)

    def say_ready(device):
        pl.semaphore_signal(ready, inc=1, device_id=device, device_id_type=MESH)

    pairs = [(shifted(q, -1), shifted(q, 1), -1) for q in QSTEPS]
    pairs += [(shifted(q, 1), shifted(q, -1), 1) for q in QSTEPS]
    pairs.append((sibling, sibling, 0))
    for t in range(7):
        for w in sorted(set(WAY[t])):
            pairs.append((chip(*w), chip(-w[0], -w[1], -w[2]), w[2]))
    for to, back, dz in pairs:
        if dz == 0:
            hello(back)
        else:
            first, last = (3, 4) if dz > 0 else (0, 7)

            @pl.when(z != last)
            def _():
                hello(back)

            @pl.when(z == first)
            def _():
                hello(to)

    def holder_of_mine(i):
        u, hy, hz = holder_of(i // 4, i % 4, cls, c)
        return device_of(u, hy, hz, c), (u == x) & (hz == z), hz >= 4

    def greet(i, _):
        device, own_place, is_late = holder_of_mine(i)

        @pl.when(jnp.logical_not(own_place) & (early | is_late))
        def _():
            hello(device)

        return 0

    def peer(i, base):
        px, pz = (x + i) % 4, base + (z + i // 4) % 4
        return device_of(px, (cls + 48 - 2 * px - 3 * pz) % 8, pz, c)

    lax.fori_loop(0, NQ * SUB, greet, 0)

    @pl.when(is_holder & early)
    def _():
        @pl.when(jnp.logical_not(is_source & (source_q == 0)))
        def _():
            hello(giver_of_mine())

        def greet_late(i, _):
            hello(peer(i, 4))
            return 0

        lax.fori_loop(0, 16, greet_late, 0)

    @pl.when(is_relay)
    def _():
        hello(source_of(1))

    def given_to(i):
        q = jnp.where(is_relay, 1, source_q)
        core = jnp.where(q == 2, 0, 1)
        k = jnp.where(is_relay, 2 * relay_no, 0) + i // 4
        u, hy, hz = holder_of(q, i % 4, k, core)
        return device_of(u, hy, hz, core)

    many = jnp.where(is_relay, 8, 32)

    @pl.when(gives)
    def _():
        def greet_given(i, _):
            hello(given_to(i))
            return 0

        lax.fori_loop(0, many, greet_given, 0)

    load = pltpu.make_async_copy(vecs, own, own_sem)

    @pl.when(is_source)
    def _():
        load.start()

    def wanted(q):
        row = gmap[pl.ds(q, 1), :]
        return row // BLK, row % BLK

    def fill_onehot(low):
        for r in range(0, BLK, 32):
            rows = lax.broadcasted_iota(jnp.int32, (32, low.shape[1]), 0) + r
            onehot[r : r + 32, :] = jnp.where(rows == low, 1.0, 0.0).astype(jnp.bfloat16)

    half = target.shape[1] // 2
    for h in range(2):
        sent[8 * h : 8 * h + 8, :half] = target[:, h * half : h * half + half].astype(jnp.float32).astype(jnp.bfloat16)
    spot = lax.broadcasted_iota(jnp.int32, (8, 8), 0) == lax.broadcasted_iota(jnp.int32, (8, 8), 1)
    spot = jnp.where(spot, jnp.broadcast_to(energy_row[...].astype(jnp.float32), (8, 8)), 0.0)
    spot = jnp.broadcast_to(jnp.sum(spot, axis=1, keepdims=True), (8, 128))
    sent[:, half:] = jnp.concatenate([spot, spot], axis=0).astype(jnp.bfloat16)
    lvl_row = band_energy[...] - (2 * occupation[...] - 1).astype(jnp.float32)
    lvl_row = lvl_row.astype(jnp.bfloat16).astype(jnp.float32)
    level[...] = jnp.broadcast_to(lvl_row, (128, 128)).T
    row_at = lax.broadcasted_iota(jnp.int32, (EXTRA, 256), 0)
    pole[...] = jnp.where(
        row_at == 0,
        freq_row[...].astype(jnp.float32),
        jnp.where(row_at == 1, weight_row[...].astype(jnp.float32), 0.0),
    ).astype(jnp.bfloat16)

    edge = (z == 0) | (z == 3)
    peers = 2 * NQ + 1 + 9
    first_held = jnp.where(c == 0, 8, 4)
    greeted_early = (
        peers
        - jnp.where(edge, 5, 0)
        + jnp.where(is_holder, 15, 0)
        + jnp.where(is_relay, 8, 0)
        + jnp.where(is_source, jnp.where(source_q == 0, 31, jnp.where(source_q == 1, 4, 32)), 0)
    )
    greeted_late = (
        peers
        + jnp.where((z == 4) | (z == 7), 5, 0)
        + first_held
        + jnp.where(is_holder, 32, 0)
    )
    greeted = jnp.where(late, greeted_late, greeted_early)
    answers = jnp.where(edge, 5, 0) + jnp.where(is_holder, 16, 0) + jnp.where(gives, many, 0)

    def target_copy(s):
        return pltpu.make_async_remote_copy(
            sent, tgt.at[s], sst.at[s], rst.at[s], device_id=shifted(QSTEPS[s], -1), device_id_type=MESH
        )

    def part_rows(u):
        return pl.ds(u * ROWS, ROWS + (EXTRA if u == SUB - 1 else 0))

    def hand_copy(q, j, u):
        core = j // 8
        hx, hy, hz = holder_of(q, u, j % 8, core)
        own_place = (hx == x) & (hy == y) & (hz == z) & (core == c)
        rows = part_rows(u)
        copy = pltpu.make_async_remote_copy(
            made.at[j, rows], held.at[q, j, rows], ss1.at[j, u], rs2.at[q, u],
            device_id=device_of(hx, hy, hz, core), device_id_type=MESH,
        )
        return copy, own_place, rows

    def hand_out(q, j):
        for u in range(SUB):
            copy, own_place, rows = hand_copy(q, j, u)

            @pl.when(jnp.logical_not(own_place))
            def _():
                copy.start()

            @pl.when(own_place)
            def _():
                pltpu.make_async_copy(made.at[j, rows], held.at[q, j, rows], rs2.at[q, u]).start()

    def handed_out(q, j):
        for u in range(SUB):
            copy, own_place, _ = hand_copy(q, j, u)

            @pl.when(jnp.logical_not(own_place))
            def _():
                copy.wait_send()

    def relay_copy(j, device):
        return pltpu.make_async_remote_copy(
            made.at[j], made.at[j], ss1.at[j, 0], rs1.at[j], device_id=device, device_id_type=MESH
        )

    @pl.when(is_source)
    def _():
        load.wait()
        high, low = wanted(source_q)
        fill_onehot(low)

        def chunk_at(pos):
            return jnp.where(source_q == 2, (pos + 8) % 16, pos)

        def prepare(pos, _):
            j = chunk_at(pos)
            mask = jnp.where(high == j, 1.0, 0.0).astype(jnp.bfloat16)
            block = lax.dot_general(
                onehot[...], own[...] * mask, (((1,), (1,)), ((), ())), preferred_element_type=jnp.float32
            )
            made[j, :BLK, :] = block.astype(jnp.bfloat16)
            made[j, BLK:, :] = pole[...]
            return 0

        def to_holders(pos, _):
            hand_out(source_q, chunk_at(pos))
            return 0

        def to_relay(pos, _):
            relay_copy(pos, relay_of(pos % 8)).start()
            return 0

        lax.fori_loop(0, AHEAD, prepare, 0)
        pl.semaphore_wait(barrier, greeted)

        @pl.when(source_q != 1)
        def _():
            lax.fori_loop(0, 8, to_holders, 0)
            lax.fori_loop(AHEAD, 16, prepare, 0)
            pl.semaphore_wait(ready, answers)
            lax.fori_loop(8, 16, to_holders, 0)

        @pl.when(source_q == 1)
        def _():
            lax.fori_loop(0, AHEAD, to_relay, 0)

            def both(pos, _):
                prepare(pos, 0)
                to_relay(pos, 0)
                return 0

            lax.fori_loop(AHEAD, 16, both, 0)

    @pl.when(jnp.logical_not(is_source))
    def _():
        pl.semaphore_wait(barrier, greeted)

    @pl.when(late)
    def _():
        def answer_holder(i, _):
            device, _, is_late = holder_of_mine(i)

            @pl.when(jnp.logical_not(is_late))
            def _():
                say_ready(device)

            return 0

        lax.fori_loop(0, NQ * SUB, answer_holder, 0)

        @pl.when(is_holder)
        def _():
            say_ready(giver_of_mine())

        for to, back, dz in pairs:
            if dz != 0:

                @pl.when(z == (4 if dz > 0 else 7))
                def _():
                    say_ready(back)

    @pl.when(z == 0)
    def _():
        pl.semaphore_wait(ready, 5)

    for s in range(NQ):
        target_copy(s).start()

    def part_copy(s, u, slot, device):
        n = ROWS + (EXTRA if u == SUB - 1 else 0)
        rows = pl.ds(u * ROWS, n)
        return pltpu.make_async_remote_copy(
            held.at[s, mine, rows], held.at[s, mine, rows], ss2.at[slot], rs2.at[s, u],
            device_id=device, device_id_type=MESH,
        )

    @pl.when(is_relay)
    def _():
        def pass_on(i, _):
            j = 2 * relay_no + i % 2 + 8 * (i // 2)

            @pl.when(i == 2)
            def _():
                pl.semaphore_wait(ready, answers)

            relay_copy(j, sibling).wait_recv()
            hand_out(1, j)
            return 0

        lax.fori_loop(0, 4, pass_on, 0)

    def give(base):
        for u in range(SUB):

            @pl.when(x == u)
            def _():
                def one(i, _):
                    part_copy(held_q, u, 4 * base + i, peer(i, base)).start()
                    return 0

                lax.fori_loop(jnp.where(late == (base == 4), 1, 0), 16, one, 0)

    @pl.when(is_holder)
    def _():
        for u in range(SUB):

            @pl.when(x == u)
            def _():
                part_copy(held_q, u, 0, sibling).wait_recv()

        give(0)

    @pl.when((z == 3) | (is_holder & early & jnp.logical_not(gives)))
    def _():
        pl.semaphore_wait(ready, answers)

    @pl.when(is_holder)
    def _():
        give(4)

    def permute_target(s, _):
        high, low = wanted(s)
        fill_onehot(low)
        pltpu.make_async_remote_copy(
            sent, tgt.at[s], sst.at[s], rst.at[s], device_id=sibling, device_id_type=MESH
        ).wait_recv()
        t = jnp.concatenate([tgt[s, :8, :half], tgt[s, 8:, :half]], axis=1).astype(jnp.float32)
        rows = jnp.concatenate([jnp.where(high == j, t, 0.0).astype(jnp.bfloat16) for j in range(16)], axis=0)
        ordered = lax.dot_general(
            rows, onehot[...], (((1,), (1,)), ((), ())), preferred_element_type=jnp.float32
        )
        for j in range(16):
            moved[s, j] = ordered[8 * j : 8 * j + 8, :]
        return 0

    def prepare_work():
        lax.fori_loop(0, NQ, permute_target, 0)
        total[...] = jnp.zeros_like(total)

    def way_to(s, t):
        if isinstance(s, int) or len(set(WAY[t])) == 1:
            return chip(*WAY[t][s if isinstance(s, int) else 0])
        return chip(*(sum(jnp.where(s == q, WAY[t][q][a], 0) for q in range(NQ)) for a in range(3)))

    def near_copy(s, t):
        return pltpu.make_async_remote_copy(
            held.at[s, mine, pl.ds(0, BLK)], held.at[s, mine, pl.ds(0, BLK)], ss3.at[s, t], rs3.at[s, cls],
            device_id=way_to(s, t), device_id_type=MESH,
        )

    def chunk_in(s, k, sem):
        j = k + 8 * c
        return pltpu.make_async_remote_copy(
            held.at[s, j, pl.ds(0, BLK)], held.at[s, j, pl.ds(0, BLK)], ss3.at[0, 0], sem,
            device_id=sibling, device_id_type=MESH,
        )

    def side_copy(s, k):
        j = k + 8 * c
        return pltpu.make_async_remote_copy(
            held.at[s, j, pl.ds(0, BLK)], held.at[s, j, pl.ds(0, BLK)], ss4.at[s, k], rs4.at[s, k],
            device_id=sibling, device_id_type=MESH,
        )

    def side_in(s, k):
        j = k + 8 * (1 - c)
        return pltpu.make_async_remote_copy(
            held.at[s, j, pl.ds(0, BLK)], held.at[s, j, pl.ds(0, BLK)], ss4.at[s, k], rs4.at[s, k],
            device_id=sibling, device_id_type=MESH,
        )

    def spread(s):
        for u in range(SUB):

            @pl.when(jnp.logical_not(is_holder & (held_q == s) & (x == u)))
            def _():
                part_copy(s, u, 0, sibling).wait_recv()

        for t in range(7):
            near_copy(s, t).start()

    def make_factor(s):
        freq = held[s, mine, BLK : BLK + EXTRA, :].astype(jnp.float32)
        f, w = freq[0:1, :], freq[1:2, :]
        wf, ff = w * f, f * f
        e = tgt[s, :, half:].astype(jnp.float32)
        lvl = level[...]
        for m in range(8):
            gap = e[m : m + 1, :] - lvl
            gap = gap * gap
            gap = jnp.concatenate([gap, gap], axis=1)
            factor[s, m * 128 : m * 128 + 128, :] = wf / (ff + gap)

    def work(s, j):
        w = waves[:, pl.ds(pl.multiple_of(j * BLK, BLK), BLK)].astype(jnp.float32)
        t = moved[s, j]
        pair = jnp.concatenate([(t[m : m + 1, :] * w).astype(jnp.bfloat16) for m in range(8)], axis=0)
        total[s] += jnp.dot(pair, held[s, j, :BLK, :], preferred_element_type=jnp.float32)

    def spread_all():
        def one(i, _):
            spread((i + 2 * c) % 3)
            return 0

        lax.fori_loop(0, NQ, one, 0)

    prepare_work()
    spread_all()
    for s in range(NQ):
        make_factor(s)

    def turn(i, _):
        s = (i + 2 * c) % 3
        other = (i + 2 - 2 * c) % 3

        def arrive(k, _):
            k = (cls + k) % 8

            @pl.when(k != cls)
            def _():
                chunk_in(s, k, rs3.at[s, k]).wait_recv()

            side_copy(s, k).start()
            work(s, k + 8 * c)
            return 0

        def arrive_side(k, _):
            k = (cls + k) % 8
            side_in(other, k).wait_recv()
            work(other, k + 8 * (1 - c))
            return 0

        lax.fori_loop(0, 8, arrive, 0)
        lax.fori_loop(0, 8, arrive_side, 0)
        return 0

    lax.fori_loop(0, NQ, turn, 0)

    def answer_copy(s):
        return pltpu.make_async_remote_copy(
            answer.at[s], part.at[s], ssr.at[s], rsr.at[s], device_id=shifted(QSTEPS[s], 1), device_id_type=MESH
        )

    for s in range(NQ):
        for m in range(8):
            rows = slice(m * 128, m * 128 + 128)
            proj = total[s, rows, :]
            answer[s, m : m + 1, :] = jnp.sum(proj * proj * factor[s, rows, :], axis=0, keepdims=True)
        answer_copy(s).start()

    for s in range(NQ):
        target_copy(s).wait_send()
        for t in range(7):
            near_copy(s, t).wait_send()

    def side_left(k, _):
        for s in range(NQ):
            side_copy(s, k).wait_send()
        return 0

    lax.fori_loop(0, 8, side_left, 0)

    @pl.when(is_holder)
    def _():
        for u in range(SUB):

            @pl.when(x == u)
            def _():
                def left(i, _):
                    @pl.when(i != jnp.where(late, 16, 0))
                    def _():
                        part_copy(held_q, u, i, sibling).wait_send()

                    return 0

                lax.fori_loop(0, 32, left, 0)

    @pl.when(is_source & (source_q != 1))
    def _():
        def left(j, _):
            handed_out(source_q, j)
            return 0

        lax.fori_loop(0, 16, left, 0)

    @pl.when(is_source & (source_q == 1))
    def _():
        def left(j, _):
            relay_copy(j, sibling).wait_send()
            return 0

        lax.fori_loop(0, 16, left, 0)

    @pl.when(is_relay)
    def _():
        def left(i, _):
            handed_out(1, 2 * relay_no + i % 2 + 8 * (i // 2))
            return 0

        lax.fori_loop(0, 4, left, 0)

    for s in range(NQ):
        answer_copy(s).wait()
    out[...] = (part[0] + part[1] + part[2]) * (1.0 / 128.0)


def local(target, target_energy, waves, band_energy, occupation, gmap, pole_vectors, pole_freq, pole_weight):
    tgt = target[0, 0, 0]
    vmem = pl.BlockSpec(memory_space=pltpu.VMEM)
    dma = pltpu.SemaphoreType.DMA
    out = pl.pallas_call(
        kernel,
        out_shape=jax.ShapeDtypeStruct((8, 256), jnp.float32),
        in_specs=[vmem, pl.BlockSpec(memory_space=pl.ANY)] + [vmem] * 7,
        out_specs=vmem,
        scratch_shapes=[
            pltpu.VMEM((NQ, 16, BLK + EXTRA, 256), jnp.bfloat16),
            pltpu.VMEM((16, BLK + EXTRA, 256), jnp.bfloat16),
            pltpu.VMEM((BLK, 4096), jnp.bfloat16),
            pltpu.VMEM((256, 4096), jnp.bfloat16),
            pltpu.VMEM((16, 2048 + 128), jnp.bfloat16),
            pltpu.VMEM((NQ, 16, 2048 + 128), jnp.bfloat16),
            pltpu.VMEM((NQ, 16, 8, BLK), jnp.float32),
            pltpu.VMEM((NQ, 1024, 256), jnp.float32),
            pltpu.VMEM((NQ, 1024, 256), jnp.float32),
            pltpu.VMEM((NQ, 8, 256), jnp.float32),
            pltpu.VMEM((NQ, 8, 256), jnp.float32),
            pltpu.VMEM((128, 128), jnp.float32),
            pltpu.VMEM((EXTRA, 256), jnp.bfloat16),
            dma,
            dma((16, SUB)),
            dma((32,)),
            dma((NQ, 7)),
            dma((NQ, 8)),
            dma((NQ,)),
            dma((NQ,)),
            dma((16,)),
            dma((NQ, SUB)),
            dma((NQ, 8)),
            dma((NQ, 8)),
            dma((NQ,)),
            dma((NQ,)),
            pltpu.SemaphoreType.REGULAR,
        ],
        compiler_params=pltpu.CompilerParams(
            collective_id=0, has_side_effects=True, vmem_limit_bytes=56 << 20
        ),
    )(
        gmap, pole_vectors[0, 0, 0], waves[0, 0, 0], tgt, target_energy[0, 0], band_energy[0, 0],
        occupation[0, 0], pole_freq[0, 0], pole_weight[0, 0],
    )
    return out[None, None, None]


def solution(mesh):
    cut = P("kx", "ky", "kz", None, None)
    row = P("kx", "ky", "kz", None)
    return jax.shard_map(
        local,
        mesh=mesh,
        in_specs=(cut, row, cut, row, row, P(), cut, row, row),
        out_specs=cut,
        check_vma=False,
    )
```

```python
import functools

import jax
import jax.numpy as jnp
from jax import lax
from jax.experimental import pallas as pl
from jax.experimental.pallas import tpu as pltpu
from jax.sharding import PartitionSpec as P

MESH = pl.DeviceIdType.MESH
QSTEPS = ((1, 0, 0), (1, 1, 0), (1, 1, 1))
NQ = 3
BLK = 256
SUB = 2
ROWS = BLK // SUB
AHEAD = 12
EXTRA = 16
NEAR = {1: (0, 1, 0), 2: (1, 0, 0), 3: (0, 0, 1), 5: (0, 0, -1), 6: (-1, 0, 0), 7: (0, -1, 0)}
FAR = ((2, 0, 0), (0, 1, 1), (0, -1, -1))
ACROSS = ((1, 1, -1), (0, 1, -3), (0, -1, 3), (-1, -1, 1))
WAY = [[FAR[s] if t == 4 else NEAR[t] for s in range(NQ)] for t in range(1, 8)]


def chip_of(me):
    kx, ky, kz = me
    return kz % 4, (ky // 2) * 2 + kz // 4, kx, ky % 2


def device_of(x, y, z, c):
    return z, (y // 2) * 2 + c, (y % 2) * 4 + x


def kernel(
    gmap, vecs, waves, target, energy_row, band_energy, occupation, freq_row, weight_row, out,
    held, made, onehot, own, sent, tgt, moved, total, factor, answer, part, level, pole,
    own_sem, ss1, ss2, ss5, rs5, ss3, ss4, sst, ssr, rs1, rs2, rs3, rs4, rst, rsr, ready,
):
    me = tuple(lax.axis_index(a) for a in ("kx", "ky", "kz"))
    x, y, z, c = chip_of(me)
    cls = (2 * x + y + 3 * z) % 8
    mine = cls + 8 * c

    def chip(dx, dy, dz, core=c):
        return device_of((x + dx + 4) % 4, (y + dy + 8) % 8, (z + dz + 8) % 8, core)

    def shifted(q, sign):
        return tuple((i + sign * d + 8) % 8 for i, d in zip(me, q))

    sibling = chip(0, 0, 0, 1 - c)
    is_source = (z == 1) & (y == 0) & ((x == 0) | ((x == 1) & (c == 1)))
    source_q = jnp.where(x == 0, c, 2)
    late = z >= 4
    early = jnp.logical_not(late)
    held_q = jnp.clip(z - 1, 0, 2)
    held_u = x % 2
    is_holder = (z >= 1) & (z <= 3) & (x // 2 == c)
    relay_no = jnp.where(z == 2, 3 - c, jnp.where(x == 3, 0, 1))
    is_relay = (y == 0) & (((x == 0) & (z == 2)) | ((z == 1) & (((x == 3) & (c == 1)) | ((x == 1) & (c == 0)))))

    def relay_of(k):
        r = k // 2
        return device_of(
            jnp.where(r == 0, 3, jnp.where(r == 1, 1, 0)),
            0,
            jnp.where(r < 2, 1, 2),
            jnp.where((r == 0) | (r == 2), 1, 0),
        )

    def source_of(s):
        return device_of(jnp.where(s == 2, 1, 0), 0, 1, jnp.where(s == 0, 0, 1))

    def holder_of(s, u, k, core):
        hx, hz = 2 * core + u, 1 + s
        return hx, (k + 48 - 2 * hx - 3 * hz) % 8, hz

    giver = tuple(jnp.where(held_q == 1, a, b) for a, b in zip(relay_of(cls), source_of(held_q)))
    from_other = is_holder & ((giver[0] != me[0]) | (giver[1] != me[1]) | (giver[2] != me[2]))
    by_z = [(z == i) | (z == j) for i, j in enumerate((7, 6, 5, 4))]
    side = jnp.where(late, -1, 1)
    partner = chip(*(side * sum(jnp.where(b, way[a], 0) for b, way in zip(by_z, ACROSS)) for a in range(3)))

    barrier = pltpu.get_barrier_semaphore()

    def hello(device):
        pl.semaphore_signal(barrier, inc=1, device_id=device, device_id_type=MESH)

    def say_ready(device):
        pl.semaphore_signal(ready, inc=1, device_id=device, device_id_type=MESH)

    pairs = [(shifted(q, -1), shifted(q, 1), -1) for q in QSTEPS]
    pairs += [(shifted(q, 1), shifted(q, -1), 1) for q in QSTEPS]
    pairs.append((sibling, sibling, 0))
    for t in range(7):
        for w in sorted(set(WAY[t])):
            pairs.append((chip(*w), chip(-w[0], -w[1], -w[2]), w[2]))
    for to, back, dz in pairs:
        if dz == 0:
            hello(back)
        else:
            first, last = (3, 4) if dz > 0 else (0, 7)

            @pl.when(z != last)
            def _():
                hello(back)

            @pl.when(z == first)
            def _():
                hello(to)

    def holder_of_mine(i):
        hx, hy, hz = holder_of(i // 2, i % 2, cls, c)
        return device_of(hx, hy, hz, c), (hx == x) & (hz == z)

    def greet(i, _):
        device, own_place = holder_of_mine(i)

        @pl.when(jnp.logical_not(own_place))
        def _():
            hello(device)

        return 0

    def peer(i):
        px, pz = (x + i) % 4, (z + i // 4) % 4
        return device_of(px, (cls + 48 - 2 * px - 3 * pz) % 8, pz, c)

    @pl.when(early)
    def _():
        lax.fori_loop(0, NQ * SUB, greet, 0)
        hello(partner)

    @pl.when(from_other)
    def _():
        hello(giver)

    @pl.when(is_relay)
    def _():
        hello(source_of(1))

    load = pltpu.make_async_copy(vecs, own, own_sem)

    @pl.when(is_source)
    def _():
        load.start()

    def wanted(q):
        row = gmap[pl.ds(q, 1), :]
        return row // BLK, row % BLK

    def fill_onehot(low):
        for r in range(0, BLK, 32):
            rows = lax.broadcasted_iota(jnp.int32, (32, low.shape[1]), 0) + r
            onehot[r : r + 32, :] = jnp.where(rows == low, 1.0, 0.0).astype(jnp.bfloat16)

    half = target.shape[1] // 2
    for h in range(2):
        sent[8 * h : 8 * h + 8, :half] = target[:, h * half : h * half + half].astype(jnp.float32).astype(jnp.bfloat16)
    spot = lax.broadcasted_iota(jnp.int32, (8, 8), 0) == lax.broadcasted_iota(jnp.int32, (8, 8), 1)
    spot = jnp.where(spot, jnp.broadcast_to(energy_row[...].astype(jnp.float32), (8, 8)), 0.0)
    spot = jnp.broadcast_to(jnp.sum(spot, axis=1, keepdims=True), (8, 128))
    sent[:, half:] = jnp.concatenate([spot, spot], axis=0).astype(jnp.bfloat16)
    lvl_row = band_energy[...] - (2 * occupation[...] - 1).astype(jnp.float32)
    lvl_row = lvl_row.astype(jnp.bfloat16).astype(jnp.float32)
    level[...] = jnp.broadcast_to(lvl_row, (128, 128)).T
    row_at = lax.broadcasted_iota(jnp.int32, (EXTRA, 256), 0)
    pole[...] = jnp.where(
        row_at == 0,
        freq_row[...].astype(jnp.float32),
        jnp.where(row_at == 1, weight_row[...].astype(jnp.float32), 0.0),
    ).astype(jnp.bfloat16)

    edge = (z == 0) | (z == 3)
    peers = 2 * NQ + 1 + 9
    greeted_early = (
        peers
        - jnp.where(edge, 5, 0)
        + jnp.where(is_holder, 15, 0)
        + jnp.where(is_relay, 8 - jnp.where(relay_no == 3, 1, 0), 0)
        + jnp.where(is_source, jnp.where(source_q == 0, 31, jnp.where(source_q == 1, 4, 32)), 0)
    )
    greeted_late = peers + jnp.where((z == 4) | (z == 7), 5, 0) + 1
    greeted = jnp.where(late, greeted_late, greeted_early)
    answers = jnp.where(edge, 5, 0) + 1

    def target_copy(s):
        return pltpu.make_async_remote_copy(
            sent, tgt.at[s], sst.at[s], rst.at[s], device_id=shifted(QSTEPS[s], -1), device_id_type=MESH
        )

    def part_rows(u):
        return pl.ds(u * ROWS, ROWS + (EXTRA if u == SUB - 1 else 0))

    def hand_copy(q, j, u):
        core = j // 8
        hx, hy, hz = holder_of(q, u, j % 8, core)
        own_place = (hx == x) & (hy == y) & (hz == z) & (core == c)
        rows = part_rows(u)
        copy = pltpu.make_async_remote_copy(
            made.at[j, rows], held.at[q, j, rows], ss1.at[j, u], rs2.at[q, u],
            device_id=device_of(hx, hy, hz, core), device_id_type=MESH,
        )
        return copy, own_place, rows

    def hand_out(q, j):
        for u in range(SUB):
            copy, own_place, rows = hand_copy(q, j, u)

            @pl.when(jnp.logical_not(own_place))
            def _():
                copy.start()

            @pl.when(own_place)
            def _():
                pltpu.make_async_copy(made.at[j, rows], held.at[q, j, rows], rs2.at[q, u]).start()

    def handed_out(q, j):
        for u in range(SUB):
            copy, own_place, _ = hand_copy(q, j, u)

            @pl.when(jnp.logical_not(own_place))
            def _():
                copy.wait_send()

    def relay_copy(j, device):
        return pltpu.make_async_remote_copy(
            made.at[j], made.at[j], ss1.at[j, 0], rs1.at[j], device_id=device, device_id_type=MESH
        )

    @pl.when(is_source)
    def _():
        load.wait()
        high, low = wanted(source_q)
        fill_onehot(low)

        def chunk_at(pos):
            return pos // 2 + 8 * (pos % 2)

        def prepare(pos, _):
            j = chunk_at(pos)
            mask = jnp.where(high == j, 1.0, 0.0).astype(jnp.bfloat16)
            block = lax.dot_general(
                onehot[...], own[...] * mask, (((1,), (1,)), ((), ())), preferred_element_type=jnp.float32
            )
            made[j, :BLK, :] = block.astype(jnp.bfloat16)
            made[j, BLK:, :] = pole[...]
            return 0

        def send(pos, _):
            j = chunk_at(pos)

            @pl.when(source_q == 1)
            def _():
                relay_copy(j, relay_of(j % 8)).start()

            @pl.when(source_q != 1)
            def _():
                hand_out(source_q, j)

            return 0

        def both(pos, _):
            prepare(pos, 0)
            send(pos, 0)
            return 0

        lax.fori_loop(0, AHEAD, prepare, 0)
        pl.semaphore_wait(barrier, greeted)
        lax.fori_loop(0, AHEAD, send, 0)
        lax.fori_loop(AHEAD, 16, both, 0)

    @pl.when(jnp.logical_not(is_source))
    def _():
        pl.semaphore_wait(barrier, greeted)

    @pl.when(late)
    def _():
        say_ready(partner)
        for to, back, dz in pairs:
            if dz != 0:

                @pl.when(z == (4 if dz > 0 else 7))
                def _():
                    say_ready(back)

    @pl.when(z == 0)
    def _():
        pl.semaphore_wait(ready, answers)

    for s in range(NQ):
        target_copy(s).start()

    def part_copy(s, u, slot, device):
        n = ROWS + (EXTRA if u == SUB - 1 else 0)
        rows = pl.ds(u * ROWS, n)
        return pltpu.make_async_remote_copy(
            held.at[s, mine, rows], held.at[s, mine, rows], ss2.at[slot], rs2.at[s, u],
            device_id=device, device_id_type=MESH,
        )

    @pl.when(is_relay)
    def _():
        def pass_on(i, _):
            j = 2 * relay_no + i // 2 + 8 * (i % 2)
            relay_copy(j, sibling).wait_recv()
            hand_out(1, j)
            return 0

        lax.fori_loop(0, 4, pass_on, 0)

    @pl.when(is_holder)
    def _():
        for u in range(SUB):

            @pl.when(held_u == u)
            def _():
                part_copy(held_q, u, 0, sibling).wait_recv()

                def give(i, _):
                    part_copy(held_q, u, i, peer(i)).start()
                    return 0

                lax.fori_loop(1, 16, give, 0)

    def permute_target(s, _):
        high, low = wanted(s)
        fill_onehot(low)
        pltpu.make_async_remote_copy(
            sent, tgt.at[s], sst.at[s], rst.at[s], device_id=sibling, device_id_type=MESH
        ).wait_recv()
        t = jnp.concatenate([tgt[s, :8, :half], tgt[s, 8:, :half]], axis=1).astype(jnp.float32)
        rows = jnp.concatenate([jnp.where(high == j, t, 0.0).astype(jnp.bfloat16) for j in range(16)], axis=0)
        ordered = lax.dot_general(
            rows, onehot[...], (((1,), (1,)), ((), ())), preferred_element_type=jnp.float32
        )
        for j in range(16):
            moved[s, j] = ordered[8 * j : 8 * j + 8, :]
        return 0

    def prepare_work():
        lax.fori_loop(0, NQ, permute_target, 0)
        total[...] = jnp.zeros_like(total)

    def way_to(s, t):
        if isinstance(s, int) or len(set(WAY[t])) == 1:
            return chip(*WAY[t][s if isinstance(s, int) else 0])
        return chip(*(sum(jnp.where(s == q, WAY[t][q][a], 0) for q in range(NQ)) for a in range(3)))

    def near_copy(s, t):
        return pltpu.make_async_remote_copy(
            held.at[s, mine, pl.ds(0, BLK)], held.at[s, mine, pl.ds(0, BLK)], ss3.at[s, t], rs3.at[s, cls],
            device_id=way_to(s, t), device_id_type=MESH,
        )

    def chunk_in(s, k, sem):
        j = k + 8 * c
        return pltpu.make_async_remote_copy(
            held.at[s, j, pl.ds(0, BLK)], held.at[s, j, pl.ds(0, BLK)], ss3.at[0, 0], sem,
            device_id=sibling, device_id_type=MESH,
        )

    def side_copy(s, k):
        j = k + 8 * c
        return pltpu.make_async_remote_copy(
            held.at[s, j, pl.ds(0, BLK)], held.at[s, j, pl.ds(0, BLK)], ss4.at[s, k], rs4.at[s, k],
            device_id=sibling, device_id_type=MESH,
        )

    def side_in(s, k):
        j = k + 8 * (1 - c)
        return pltpu.make_async_remote_copy(
            held.at[s, j, pl.ds(0, BLK)], held.at[s, j, pl.ds(0, BLK)], ss4.at[s, k], rs4.at[s, k],
            device_id=sibling, device_id_type=MESH,
        )

    def across_copy(s):
        return pltpu.make_async_remote_copy(
            held.at[s, mine], held.at[s, mine], ss5.at[s], rs5.at[s], device_id=partner, device_id_type=MESH
        )

    def spread(s):
        @pl.when(late)
        def _():
            across_copy(s).wait_recv()

        @pl.when(early)
        def _():
            for u in range(SUB):

                @pl.when(jnp.logical_not(is_holder & (held_q == s) & (held_u == u)))
                def _():
                    part_copy(s, u, 0, sibling).wait_recv()

            across_copy(s).start()

        for t in range(7):
            near_copy(s, t).start()

    def make_factor(s):
        freq = held[s, mine, BLK : BLK + EXTRA, :].astype(jnp.float32)
        f, w = freq[0:1, :], freq[1:2, :]
        wf, ff = w * f, f * f
        e = tgt[s, :, half:].astype(jnp.float32)
        lvl = level[...]
        for m in range(8):
            gap = e[m : m + 1, :] - lvl
            gap = gap * gap
            gap = jnp.concatenate([gap, gap], axis=1)
            factor[s, m * 128 : m * 128 + 128, :] = wf / (ff + gap)

    def work(s, j):
        w = waves[:, pl.ds(pl.multiple_of(j * BLK, BLK), BLK)].astype(jnp.float32)
        t = moved[s, j]
        pair = jnp.concatenate([(t[m : m + 1, :] * w).astype(jnp.bfloat16) for m in range(8)], axis=0)
        total[s] += jnp.dot(pair, held[s, j, :BLK, :], preferred_element_type=jnp.float32)

    def spread_all():
        def one(i, _):
            spread((2 * i) % 3)
            return 0

        lax.fori_loop(0, NQ, one, 0)

    prepare_work()

    @pl.when(early & (z != 0))
    def _():
        pl.semaphore_wait(ready, answers)

    spread_all()
    for s in range(NQ):
        make_factor(s)

    def turn(i, _):
        s = (2 * i) % 3

        def arrive(k, _):
            k = (cls + k) % 8

            @pl.when(k != cls)
            def _():
                chunk_in(s, k, rs3.at[s, k]).wait_recv()

            side_copy(s, k).start()
            work(s, k + 8 * c)
            return 0

        def arrive_side(k, _):
            k = (cls + k) % 8
            side_in(s, k).wait_recv()
            work(s, k + 8 * (1 - c))
            return 0

        lax.fori_loop(0, 8, arrive, 0)
        lax.fori_loop(0, 8, arrive_side, 0)
        return 0

    lax.fori_loop(0, NQ, turn, 0)

    def answer_copy(s):
        return pltpu.make_async_remote_copy(
            answer.at[s], part.at[s], ssr.at[s], rsr.at[s], device_id=shifted(QSTEPS[s], 1), device_id_type=MESH
        )

    for s in range(NQ):
        for m in range(8):
            rows = slice(m * 128, m * 128 + 128)
            proj = total[s, rows, :]
            answer[s, m : m + 1, :] = jnp.sum(proj * proj * factor[s, rows, :], axis=0, keepdims=True)
        answer_copy(s).start()

    for s in range(NQ):
        target_copy(s).wait_send()
        for t in range(7):
            near_copy(s, t).wait_send()

    def side_left(k, _):
        for s in range(NQ):
            side_copy(s, k).wait_send()
        return 0

    lax.fori_loop(0, 8, side_left, 0)

    @pl.when(early)
    def _():
        for s in range(NQ):
            across_copy(s).wait_send()

    @pl.when(is_holder)
    def _():
        for u in range(SUB):

            @pl.when(held_u == u)
            def _():
                def left(i, _):
                    part_copy(held_q, u, i, sibling).wait_send()
                    return 0

                lax.fori_loop(1, 16, left, 0)

    @pl.when(is_source & (source_q != 1))
    def _():
        def left(j, _):
            handed_out(source_q, j)
            return 0

        lax.fori_loop(0, 16, left, 0)

    @pl.when(is_source & (source_q == 1))
    def _():
        def left(j, _):
            relay_copy(j, sibling).wait_send()
            return 0

        lax.fori_loop(0, 16, left, 0)

    @pl.when(is_relay)
    def _():
        def left(i, _):
            handed_out(1, 2 * relay_no + i // 2 + 8 * (i % 2))
            return 0

        lax.fori_loop(0, 4, left, 0)

    for s in range(NQ):
        answer_copy(s).wait()
    out[...] = (part[0] + part[1] + part[2]) * (1.0 / 128.0)


def local(target, target_energy, waves, band_energy, occupation, gmap, pole_vectors, pole_freq, pole_weight):
    tgt = target[0, 0, 0]
    vmem = pl.BlockSpec(memory_space=pltpu.VMEM)
    dma = pltpu.SemaphoreType.DMA
    out = pl.pallas_call(
        kernel,
        out_shape=jax.ShapeDtypeStruct((8, 256), jnp.float32),
        in_specs=[vmem, pl.BlockSpec(memory_space=pl.ANY)] + [vmem] * 7,
        out_specs=vmem,
        scratch_shapes=[
            pltpu.VMEM((NQ, 16, BLK + EXTRA, 256), jnp.bfloat16),
            pltpu.VMEM((16, BLK + EXTRA, 256), jnp.bfloat16),
            pltpu.VMEM((BLK, 4096), jnp.bfloat16),
            pltpu.VMEM((256, 4096), jnp.bfloat16),
            pltpu.VMEM((16, 2048 + 128), jnp.bfloat16),
            pltpu.VMEM((NQ, 16, 2048 + 128), jnp.bfloat16),
            pltpu.VMEM((NQ, 16, 8, BLK), jnp.float32),
            pltpu.VMEM((NQ, 1024, 256), jnp.float32),
            pltpu.VMEM((NQ, 1024, 256), jnp.float32),
            pltpu.VMEM((NQ, 8, 256), jnp.float32),
            pltpu.VMEM((NQ, 8, 256), jnp.float32),
            pltpu.VMEM((128, 128), jnp.float32),
            pltpu.VMEM((EXTRA, 256), jnp.bfloat16),
            dma,
            dma((16, SUB)),
            dma((16,)),
            dma((NQ,)),
            dma((NQ,)),
            dma((NQ, 7)),
            dma((NQ, 8)),
            dma((NQ,)),
            dma((NQ,)),
            dma((16,)),
            dma((NQ, SUB)),
            dma((NQ, 8)),
            dma((NQ, 8)),
            dma((NQ,)),
            dma((NQ,)),
            pltpu.SemaphoreType.REGULAR,
        ],
        compiler_params=pltpu.CompilerParams(
            collective_id=0, has_side_effects=True, vmem_limit_bytes=56 << 20
        ),
    )(
        gmap, pole_vectors[0, 0, 0], waves[0, 0, 0], tgt, target_energy[0, 0], band_energy[0, 0],
        occupation[0, 0], pole_freq[0, 0], pole_weight[0, 0],
    )
    return out[None, None, None]


def solution(mesh):
    cut = P("kx", "ky", "kz", None, None)
    row = P("kx", "ky", "kz", None)
    return jax.shard_map(
        local,
        mesh=mesh,
        in_specs=(cut, row, cut, row, row, P(), cut, row, row),
        out_specs=cut,
        check_vma=False,
    )
```

```python
import functools

import jax
import jax.numpy as jnp
from jax import lax
from jax.experimental import pallas as pl
from jax.experimental.pallas import tpu as pltpu
from jax.sharding import PartitionSpec as P

MESH = pl.DeviceIdType.MESH
QSTEPS = ((1, 0, 0), (1, 1, 0), (1, 1, 1))
NQ = 3
BLK = 256
SUB = 4
ROWS = BLK // SUB
AHEAD = 8
EXTRA = 16
NEAR = {1: (0, 1, 0), 2: (1, 0, 0), 3: (0, 0, 1), 5: (0, 0, -1), 6: (-1, 0, 0), 7: (0, -1, 0)}
FAR = ((2, 0, 0), (0, 1, 1), (0, -1, -1))
WAY = [[FAR[s] if t == 4 else NEAR[t] for s in range(NQ)] for t in range(1, 8)]


def chip_of(me):
    kx, ky, kz = me
    return kz % 4, (ky // 2) * 2 + kz // 4, kx, ky % 2


def device_of(x, y, z, c):
    return z, (y // 2) * 2 + c, (y % 2) * 4 + x


def kernel(
    gmap, vecs, waves, target, energy_row, band_energy, occupation, freq_row, weight_row, out,
    held, made, onehot, own, sent, tgt, moved, total, factor, answer, part, level, pole,
    own_sem, ss1, ss2, ss3, ss4, sst, ssr, rs1, rs2, rs3, rs4, rst, rsr, ready,
):
    me = tuple(lax.axis_index(a) for a in ("kx", "ky", "kz"))
    x, y, z, c = chip_of(me)
    cls = (2 * x + y + 3 * z) % 8
    mine = cls + 8 * c

    def chip(dx, dy, dz, core=c):
        return device_of((x + dx + 4) % 4, (y + dy + 8) % 8, (z + dz + 8) % 8, core)

    def shifted(q, sign):
        return tuple((i + sign * d + 8) % 8 for i, d in zip(me, q))

    sibling = chip(0, 0, 0, 1 - c)
    is_source = (z == 1) & (y == 0) & ((x == 0) | ((x == 1) & (c == 1)))
    source_q = jnp.where(x == 0, c, 2)
    late = z >= 4
    early = jnp.logical_not(late)
    held_at = (z + 7 - 4 * c) % 8
    held_q = jnp.minimum(held_at // 2, 2)
    is_holder = (held_at == 0) | (held_at == 2) | (held_at == 5)
    relay_no = jnp.where(z == 2, 3 - c, jnp.where(x == 3, 0, 1))
    is_relay = (y == 0) & (((x == 0) & (z == 2)) | ((z == 1) & (((x == 3) & (c == 1)) | ((x == 1) & (c == 0)))))
    gives = (is_source & (source_q != 1)) | is_relay

    def first_z(s, core):
        return (1 + 2 * s + s // 2 + 4 * core) % 8

    def relay_of(k):
        r = k // 2
        return device_of(
            jnp.where(r == 0, 3, jnp.where(r == 1, 1, 0)),
            0,
            jnp.where(r < 2, 1, 2),
            jnp.where((r == 0) | (r == 2), 1, 0),
        )

    def source_of(s):
        return device_of(jnp.where(s == 2, 1, 0), 0, 1, jnp.where(s == 0, 0, 1))

    def holder_of(s, u, k, core):
        hz = first_z(s, core)
        return u, (k + 48 - 2 * u - 3 * hz) % 8, hz

    def giver_of_mine():
        to_relay = held_q == 1
        return tuple(jnp.where(to_relay, a, b) for a, b in zip(relay_of(cls), source_of(held_q)))

    barrier = pltpu.get_barrier_semaphore()

    def hello(device):
        pl.semaphore_signal(barrier, inc=1, device_id=device, device_id_type=MESH)

    def say_ready(device):
        pl.semaphore_signal(ready, inc=1, device_id=device, device_id_type=MESH)

    pairs = [(shifted(q, -1), shifted(q, 1), -1) for q in QSTEPS]
    pairs += [(shifted(q, 1), shifted(q, -1), 1) for q in QSTEPS]
    pairs.append((sibling, sibling, 0))
    for t in range(7):
        for w in sorted(set(WAY[t])):
            pairs.append((chip(*w), chip(-w[0], -w[1], -w[2]), w[2]))
    for to, back, dz in pairs:
        if dz == 0:
            hello(back)
        else:
            first, last = (3, 4) if dz > 0 else (0, 7)

            @pl.when(z != last)
            def _():
                hello(back)

            @pl.when(z == first)
            def _():
                hello(to)

    def holder_of_mine(i):
        u, hy, hz = holder_of(i // 4, i % 4, cls, c)
        return device_of(u, hy, hz, c), (u == x) & (hz == z), hz >= 4

    def greet(i, _):
        device, own_place, is_late = holder_of_mine(i)

        @pl.when(jnp.logical_not(own_place) & (early | is_late))
        def _():
            hello(device)

        return 0

    def peer(i, base):
        px, pz = (x + i) % 4, base + (z + i // 4) % 4
        return device_of(px, (cls + 48 - 2 * px - 3 * pz) % 8, pz, c)

    lax.fori_loop(0, NQ * SUB, greet, 0)

    @pl.when(is_holder & early)
    def _():
        @pl.when(jnp.logical_not(is_source & (source_q == 0)))
        def _():
            hello(giver_of_mine())

        def greet_late(i, _):
            hello(peer(i, 4))
            return 0

        lax.fori_loop(0, 16, greet_late, 0)

    @pl.when(is_relay)
    def _():
        hello(source_of(1))

    def given_to(i):
        q = jnp.where(is_relay, 1, source_q)
        core = jnp.where(q == 2, 0, 1)
        k = jnp.where(is_relay, 2 * relay_no, 0) + i // 4
        u, hy, hz = holder_of(q, i % 4, k, core)
        return device_of(u, hy, hz, core)

    many = jnp.where(is_relay, 8, 32)

    @pl.when(gives)
    def _():
        def greet_given(i, _):
            hello(given_to(i))
            return 0

        lax.fori_loop(0, many, greet_given, 0)

    edge = (z == 0) | (z == 3)
    peers = 2 * NQ + 1 + 9
    first_held = jnp.where(c == 0, 8, 4)
    greeted_early = (
        peers
        - jnp.where(edge, 5, 0)
        + jnp.where(is_holder, 15, 0)
        + jnp.where(is_relay, 8, 0)
        + jnp.where(is_source, jnp.where(source_q == 0, 31, jnp.where(source_q == 1, 4, 32)), 0)
    )
    greeted_late = (
        peers
        + jnp.where((z == 4) | (z == 7), 5, 0)
        + first_held
        + jnp.where(is_holder, 32, 0)
    )
    greeted = jnp.where(late, greeted_late, greeted_early)
    answers = jnp.where(edge, 5, 0) + jnp.where(is_holder, 16, 0) + jnp.where(gives, many, 0)

    @pl.when(late)
    def _():
        pl.semaphore_wait(barrier, greeted)

        @pl.when(is_holder)
        def _():
            say_ready(giver_of_mine())

        def answer_holder(i, _):
            device, _, is_late = holder_of_mine(i)

            @pl.when(jnp.logical_not(is_late))
            def _():
                say_ready(device)

            return 0

        lax.fori_loop(0, NQ * SUB, answer_holder, 0)

        for to, back, dz in pairs:
            if dz != 0:

                @pl.when(z == (4 if dz > 0 else 7))
                def _():
                    say_ready(back)

    load = pltpu.make_async_copy(vecs, own, own_sem)

    @pl.when(is_source)
    def _():
        load.start()

    def wanted(q):
        row = gmap[pl.ds(q, 1), :]
        return row // BLK, row % BLK

    def fill_onehot(low):
        for r in range(0, BLK, 32):
            rows = lax.broadcasted_iota(jnp.int32, (32, low.shape[1]), 0) + r
            onehot[r : r + 32, :] = jnp.where(rows == low, 1.0, 0.0).astype(jnp.bfloat16)

    half = target.shape[1] // 2
    for h in range(2):
        sent[8 * h : 8 * h + 8, :half] = target[:, h * half : h * half + half].astype(jnp.float32).astype(jnp.bfloat16)
    spot = lax.broadcasted_iota(jnp.int32, (8, 8), 0) == lax.broadcasted_iota(jnp.int32, (8, 8), 1)
    spot = jnp.where(spot, jnp.broadcast_to(energy_row[...].astype(jnp.float32), (8, 8)), 0.0)
    spot = jnp.broadcast_to(jnp.sum(spot, axis=1, keepdims=True), (8, 128))
    sent[:, half:] = jnp.concatenate([spot, spot], axis=0).astype(jnp.bfloat16)
    lvl_row = band_energy[...] - (2 * occupation[...] - 1).astype(jnp.float32)
    lvl_row = lvl_row.astype(jnp.bfloat16).astype(jnp.float32)
    level[...] = jnp.broadcast_to(lvl_row, (128, 128)).T
    row_at = lax.broadcasted_iota(jnp.int32, (EXTRA, 256), 0)
    pole[...] = jnp.where(
        row_at == 0,
        freq_row[...].astype(jnp.float32),
        jnp.where(row_at == 1, weight_row[...].astype(jnp.float32), 0.0),
    ).astype(jnp.bfloat16)

    def target_copy(s):
        return pltpu.make_async_remote_copy(
            sent, tgt.at[s], sst.at[s], rst.at[s], device_id=shifted(QSTEPS[s], -1), device_id_type=MESH
        )

    def part_rows(u):
        return pl.ds(u * ROWS, ROWS + (EXTRA if u == SUB - 1 else 0))

    def hand_copy(q, j, u):
        core = j // 8
        hx, hy, hz = holder_of(q, u, j % 8, core)
        own_place = (hx == x) & (hy == y) & (hz == z) & (core == c)
        rows = part_rows(u)
        copy = pltpu.make_async_remote_copy(
            made.at[j, rows], held.at[q, j, rows], ss1.at[j, u], rs2.at[q, u],
            device_id=device_of(hx, hy, hz, core), device_id_type=MESH,
        )
        return copy, own_place, rows

    def hand_out(q, j):
        for u in range(SUB):
            copy, own_place, rows = hand_copy(q, j, u)

            @pl.when(jnp.logical_not(own_place))
            def _():
                copy.start()

            @pl.when(own_place)
            def _():
                pltpu.make_async_copy(made.at[j, rows], held.at[q, j, rows], rs2.at[q, u]).start()

    def handed_out(q, j):
        for u in range(SUB):
            copy, own_place, _ = hand_copy(q, j, u)

            @pl.when(jnp.logical_not(own_place))
            def _():
                copy.wait_send()

    def relay_copy(j, device):
        return pltpu.make_async_remote_copy(
            made.at[j], made.at[j], ss1.at[j, 0], rs1.at[j], device_id=device, device_id_type=MESH
        )

    @pl.when(is_source)
    def _():
        load.wait()
        high, low = wanted(source_q)
        fill_onehot(low)

        def chunk_at(pos):
            return jnp.where(source_q == 2, (pos + 8) % 16, pos)

        def prepare(pos, _):
            j = chunk_at(pos)
            mask = jnp.where(high == j, 1.0, 0.0).astype(jnp.bfloat16)
            block = lax.dot_general(
                onehot[...], own[...] * mask, (((1,), (1,)), ((), ())), preferred_element_type=jnp.float32
            )
            made[j, :BLK, :] = block.astype(jnp.bfloat16)
            made[j, BLK:, :] = pole[...]
            return 0

        def to_holders(pos, _):
            hand_out(source_q, chunk_at(pos))
            return 0

        def to_relay(pos, _):
            relay_copy(pos, relay_of(pos % 8)).start()
            return 0

        lax.fori_loop(0, AHEAD, prepare, 0)
        pl.semaphore_wait(barrier, greeted)

        @pl.when(source_q != 1)
        def _():
            lax.fori_loop(0, 8, to_holders, 0)
            lax.fori_loop(AHEAD, 16, prepare, 0)
            pl.semaphore_wait(ready, answers)
            lax.fori_loop(8, 16, to_holders, 0)

        @pl.when(source_q == 1)
        def _():
            lax.fori_loop(0, AHEAD, to_relay, 0)

            def both(pos, _):
                prepare(pos, 0)
                to_relay(pos, 0)
                return 0

            lax.fori_loop(AHEAD, 16, both, 0)

    @pl.when(early & jnp.logical_not(is_source))
    def _():
        pl.semaphore_wait(barrier, greeted)

    @pl.when(z == 0)
    def _():
        pl.semaphore_wait(ready, 5)

    for s in range(NQ):
        target_copy(s).start()

    def part_copy(s, u, slot, device):
        n = ROWS + (EXTRA if u == SUB - 1 else 0)
        rows = pl.ds(u * ROWS, n)
        return pltpu.make_async_remote_copy(
            held.at[s, mine, rows], held.at[s, mine, rows], ss2.at[slot], rs2.at[s, u],
            device_id=device, device_id_type=MESH,
        )

    @pl.when(is_relay)
    def _():
        def pass_on(i, _):
            j = 2 * relay_no + i % 2 + 8 * (i // 2)

            @pl.when(i == 2)
            def _():
                pl.semaphore_wait(ready, answers)

            relay_copy(j, sibling).wait_recv()
            hand_out(1, j)
            return 0

        lax.fori_loop(0, 4, pass_on, 0)

    def give(base):
        for u in range(SUB):

            @pl.when(x == u)
            def _():
                def one(i, _):
                    part_copy(held_q, u, 4 * base + i, peer(i, base)).start()
                    return 0

                lax.fori_loop(jnp.where(late == (base == 4), 1, 0), 16, one, 0)

    @pl.when(is_holder)
    def _():
        for u in range(SUB):

            @pl.when(x == u)
            def _():
                part_copy(held_q, u, 0, sibling).wait_recv()

        give(0)

    @pl.when((z == 3) | (is_holder & early & jnp.logical_not(gives)))
    def _():
        pl.semaphore_wait(ready, answers)

    @pl.when(is_holder)
    def _():
        give(4)

    def permute_target(s, _):
        high, low = wanted(s)
        fill_onehot(low)
        pltpu.make_async_remote_copy(
            sent, tgt.at[s], sst.at[s], rst.at[s], device_id=sibling, device_id_type=MESH
        ).wait_recv()
        t = jnp.concatenate([tgt[s, :8, :half], tgt[s, 8:, :half]], axis=1).astype(jnp.float32)
        rows = jnp.concatenate([jnp.where(high == j, t, 0.0).astype(jnp.bfloat16) for j in range(16)], axis=0)
        ordered = lax.dot_general(
            rows, onehot[...], (((1,), (1,)), ((), ())), preferred_element_type=jnp.float32
        )
        for j in range(16):
            moved[s, j] = ordered[8 * j : 8 * j + 8, :]
        return 0

    def prepare_work():
        lax.fori_loop(0, NQ, permute_target, 0)
        total[...] = jnp.zeros_like(total)

    def way_to(s, t):
        if isinstance(s, int) or len(set(WAY[t])) == 1:
            return chip(*WAY[t][s if isinstance(s, int) else 0])
        return chip(*(sum(jnp.where(s == q, WAY[t][q][a], 0) for q in range(NQ)) for a in range(3)))

    def near_copy(s, t):
        return pltpu.make_async_remote_copy(
            held.at[s, mine, pl.ds(0, BLK)], held.at[s, mine, pl.ds(0, BLK)], ss3.at[s, t], rs3.at[s, cls],
            device_id=way_to(s, t), device_id_type=MESH,
        )

    def chunk_in(s, k, sem):
        j = k + 8 * c
        return pltpu.make_async_remote_copy(
            held.at[s, j, pl.ds(0, BLK)], held.at[s, j, pl.ds(0, BLK)], ss3.at[0, 0], sem,
            device_id=sibling, device_id_type=MESH,
        )

    def side_copy(s, k):
        j = k + 8 * c
        return pltpu.make_async_remote_copy(
            held.at[s, j, pl.ds(0, BLK)], held.at[s, j, pl.ds(0, BLK)], ss4.at[s, k], rs4.at[s, k],
            device_id=sibling, device_id_type=MESH,
        )

    def side_in(s, k):
        j = k + 8 * (1 - c)
        return pltpu.make_async_remote_copy(
            held.at[s, j, pl.ds(0, BLK)], held.at[s, j, pl.ds(0, BLK)], ss4.at[s, k], rs4.at[s, k],
            device_id=sibling, device_id_type=MESH,
        )

    def spread(s):
        for u in range(SUB):

            @pl.when(jnp.logical_not(is_holder & (held_q == s) & (x == u)))
            def _():
                part_copy(s, u, 0, sibling).wait_recv()

        for t in range(7):
            near_copy(s, t).start()

    def make_factor(s):
        freq = held[s, mine, BLK : BLK + EXTRA, :].astype(jnp.float32)
        f, w = freq[0:1, :], freq[1:2, :]
        wf, ff = w * f, f * f
        e = tgt[s, :, half:].astype(jnp.float32)
        lvl = level[...]
        for m in range(8):
            gap = e[m : m + 1, :] - lvl
            gap = gap * gap
            gap = jnp.concatenate([gap, gap], axis=1)
            factor[s, m * 128 : m * 128 + 128, :] = wf / (ff + gap)

    def work(s, j):
        w = waves[:, pl.ds(pl.multiple_of(j * BLK, BLK), BLK)]
        t = moved[s, j].astype(jnp.bfloat16)
        pair = jnp.concatenate([t[m : m + 1, :] * w for m in range(8)], axis=0)
        total[s] += jnp.dot(pair, held[s, j, :BLK, :], preferred_element_type=jnp.float32)

    def spread_all():
        def one(i, _):
            spread((2 * i) % 3)
            return 0

        lax.fori_loop(0, NQ, one, 0)

    prepare_work()
    spread_all()
    for s in range(NQ):
        make_factor(s)

    def answer_copy(s):
        return pltpu.make_async_remote_copy(
            answer.at[s], part.at[s], ssr.at[s], rsr.at[s], device_id=shifted(QSTEPS[s], 1), device_id_type=MESH
        )

    def turn(i, _):
        s = (2 * i) % 3

        def arrive(k, _):
            k = (cls + k) % 8

            @pl.when(k != cls)
            def _():
                chunk_in(s, k, rs3.at[s, k]).wait_recv()

            side_copy(s, k).start()
            work(s, k + 8 * c)
            return 0

        def arrive_side(k, _):
            k = (cls + k) % 8
            side_in(s, k).wait_recv()
            work(s, k + 8 * (1 - c))
            return 0

        lax.fori_loop(0, 8, arrive, 0)
        lax.fori_loop(0, 8, arrive_side, 0)
        for q in range(NQ):

            @pl.when(s == q)
            def _():
                for m in range(8):
                    rows = slice(m * 128, m * 128 + 128)
                    proj = total[q, rows, :]
                    answer[q, m : m + 1, :] = jnp.sum(proj * proj * factor[q, rows, :], axis=0, keepdims=True)
                answer_copy(q).start()

        return 0

    lax.fori_loop(0, NQ, turn, 0)

    for s in range(NQ):
        target_copy(s).wait_send()
        for t in range(7):
            near_copy(s, t).wait_send()

    def side_left(k, _):
        for s in range(NQ):
            side_copy(s, k).wait_send()
        return 0

    lax.fori_loop(0, 8, side_left, 0)

    @pl.when(is_holder)
    def _():
        for u in range(SUB):

            @pl.when(x == u)
            def _():
                def left(i, _):
                    @pl.when(i != jnp.where(late, 16, 0))
                    def _():
                        part_copy(held_q, u, i, sibling).wait_send()

                    return 0

                lax.fori_loop(0, 32, left, 0)

    @pl.when(is_source & (source_q != 1))
    def _():
        def left(j, _):
            handed_out(source_q, j)
            return 0

        lax.fori_loop(0, 16, left, 0)

    @pl.when(is_source & (source_q == 1))
    def _():
        def left(j, _):
            relay_copy(j, sibling).wait_send()
            return 0

        lax.fori_loop(0, 16, left, 0)

    @pl.when(is_relay)
    def _():
        def left(i, _):
            handed_out(1, 2 * relay_no + i % 2 + 8 * (i // 2))
            return 0

        lax.fori_loop(0, 4, left, 0)

    for s in range(NQ):
        answer_copy(s).wait()
    out[...] = (part[0] + part[1] + part[2]) * (1.0 / 128.0)


def local(target, target_energy, waves, band_energy, occupation, gmap, pole_vectors, pole_freq, pole_weight):
    tgt = target[0, 0, 0]
    vmem = pl.BlockSpec(memory_space=pltpu.VMEM)
    dma = pltpu.SemaphoreType.DMA
    out = pl.pallas_call(
        kernel,
        out_shape=jax.ShapeDtypeStruct((8, 256), jnp.float32),
        in_specs=[vmem, pl.BlockSpec(memory_space=pl.ANY)] + [vmem] * 7,
        out_specs=vmem,
        scratch_shapes=[
            pltpu.VMEM((NQ, 16, BLK + EXTRA, 256), jnp.bfloat16),
            pltpu.VMEM((16, BLK + EXTRA, 256), jnp.bfloat16),
            pltpu.VMEM((BLK, 4096), jnp.bfloat16),
            pltpu.VMEM((256, 4096), jnp.bfloat16),
            pltpu.VMEM((16, 2048 + 128), jnp.bfloat16),
            pltpu.VMEM((NQ, 16, 2048 + 128), jnp.bfloat16),
            pltpu.VMEM((NQ, 16, 8, BLK), jnp.float32),
            pltpu.VMEM((NQ, 1024, 256), jnp.float32),
            pltpu.VMEM((NQ, 1024, 256), jnp.float32),
            pltpu.VMEM((NQ, 8, 256), jnp.float32),
            pltpu.VMEM((NQ, 8, 256), jnp.float32),
            pltpu.VMEM((128, 128), jnp.float32),
            pltpu.VMEM((EXTRA, 256), jnp.bfloat16),
            dma,
            dma((16, SUB)),
            dma((32,)),
            dma((NQ, 7)),
            dma((NQ, 8)),
            dma((NQ,)),
            dma((NQ,)),
            dma((16,)),
            dma((NQ, SUB)),
            dma((NQ, 8)),
            dma((NQ, 8)),
            dma((NQ,)),
            dma((NQ,)),
            pltpu.SemaphoreType.REGULAR,
        ],
        compiler_params=pltpu.CompilerParams(
            collective_id=0, has_side_effects=True, vmem_limit_bytes=56 << 20
        ),
    )(
        gmap, pole_vectors[0, 0, 0], waves[0, 0, 0], tgt, target_energy[0, 0], band_energy[0, 0],
        occupation[0, 0], pole_freq[0, 0], pole_weight[0, 0],
    )
    return out[None, None, None]


def solution(mesh):
    cut = P("kx", "ky", "kz", None, None)
    row = P("kx", "ky", "kz", None)
    return jax.shard_map(
        local,
        mesh=mesh,
        in_specs=(cut, row, cut, row, row, P(), cut, row, row),
        out_specs=cut,
        check_vma=False,
    )
```
